128 devices in a mesh: ctx: 8 (over z, core), work: 16 (over y, x).
Axes of the slice: x: 4, y: 4, z: 4, core: 2. Of those that a mesh axis runs over, the one named last changes fastest.
Arguments:
- query_states: bfloat16 [4, 8192, 4096], P(None, ('ctx', 'work')), may hold values from -6 to 6
- key_states: bfloat16 [4, 8192, 256], P(None, ('ctx', 'work')), may hold values from -12 to 12
- value_states: bfloat16 [4, 8192, 256], P(None, ('ctx', 'work')), may hold values from -6 to 6
- forward_out: bfloat16 [4, 8192, 4096], P(None, ('ctx', 'work')), may hold values from -4 to 4
- out_grad: bfloat16 [4, 8192, 4096], P(None, ('ctx', 'work')), may hold values from -6 to 6
- log_norm: float32 [4, 8192, 32], P(None, ('ctx', 'work')), may hold values from 3 to 5
- selected: int32 [4, 128, 2, 15], P(None, ('ctx', 'work')), may hold values from -1 to 511, as said below
Outputs:
- query_grad: bfloat16 [4, 8192, 4096], P(None, ('ctx', 'work'))
- key_grad: bfloat16 [4, 8192, 256], P(None, ('ctx', 'work'))
- value_grad: bfloat16 [4, 8192, 256], P(None, ('ctx', 'work'))
The draws below stay inside these ranges and needn't reach their ends.
Inputs may be any that keep to these rules, and one draw needn't show every extreme that they name: selected[r, d, g] lists the blocks that query block r * 128 + d selects for key-value head g: distinct blocks strictly before it, or -1 for an empty entry. Block b belongs to device b mod 128 of ctx+work. The nonempty entries of all lists of one device name at most 1 block of any one device, and some device reaches 1.
All inputs are finite; a program needn't handle non-finite values.
Results may differ from the reference program's by a relative error of at most 0.0049.
Values may be sent and summed in bfloat16 or wider, within the bound.
No kernel may reach another device: no remote copies, remote signals or barrier semaphores. Data moves between devices by JAX's collectives and lax.ppermute only.
A program may use at most 128 MiB of HBM per device.

```python
import math
import jax
import jax.numpy as jnp
from jax import lax

HD = 128
KVH = 2
GQ = 16
QH = 32
BLK = 64
NSEL = 15
R = 4
ROUND_TOKENS = 8192
N_CTX = 8
N_WORK = 16


def block_directions(key):
    base = jax.random.fold_in(key, 11)
    direction_key, level_key = jax.random.split(base)
    directions = jax.random.truncated_normal(direction_key, -4.0, 4.0, (R, N_CTX * N_WORK, KVH, HD), jnp.float32)
    levels = jax.random.uniform(level_key, (R, N_CTX * N_WORK, KVH), jnp.float32, 1.0, 4.0)
    return (directions, levels)


def draw_query_states(key, part):
    directions, levels = block_directions(key)
    key = jax.random.fold_in(key, 3)
    round_blocks = N_CTX * N_WORK
    noise = jax.random.truncated_normal(key, -4.0, 4.0, (R, round_blocks, BLK, KVH, GQ, HD), jnp.float32)
    shared = directions[:, :, None, :, None, :]
    queries = 0.6 * shared + 0.8 * noise
    return queries.reshape(R, round_blocks * BLK, KVH * GQ * HD).astype(jnp.bfloat16)


def draw_key_states(key, part):
    directions, levels = block_directions(key)
    key = jax.random.fold_in(key, 5)
    round_blocks = N_CTX * N_WORK
    noise = jax.random.truncated_normal(key, -4.0, 4.0, (R, round_blocks, BLK, KVH, HD), jnp.float32)
    strength = levels / (0.6 * math.sqrt(HD))
    leading = strength[..., None] * directions
    first_token = (jnp.arange(BLK, dtype=jnp.int32) == 0)[None, None, :, None, None]
    keys = jnp.where(first_token, leading[:, :, None, :, :], noise)
    return keys.reshape(R, round_blocks * BLK, KVH * HD).astype(jnp.bfloat16)


def draw_out_grad(key, part):
    key = jax.random.fold_in(key, 9)
    common_key, noise_key = jax.random.split(key)
    width = KVH * GQ * HD
    tokens = N_CTX * N_WORK * BLK
    common = jax.random.truncated_normal(common_key, -4.0, 4.0, (width,), jnp.float32)
    noise = jax.random.truncated_normal(noise_key, -4.0, 4.0, (R, tokens, width), jnp.float32)
    return (0.7 * common[None, None, :] + 0.7 * noise).astype(jnp.bfloat16)


def draw_selected(key, part):
    key = jax.random.fold_in(key, 7)
    device_count = N_CTX * N_WORK
    item_count = R * KVH * NSEL
    order_key, round_key = jax.random.split(key)
    orderings = jax.vmap(lambda single: jax.random.permutation(single, device_count))(jax.random.split(order_key, device_count))
    owner_ids = orderings[:, jnp.arange(item_count) % device_count].astype(jnp.int32)
    owner_ids = jnp.transpose(owner_ids.reshape(device_count, R, KVH, NSEL), (1, 0, 2, 3))
    round_index = jnp.arange(R, dtype=jnp.int32)[:, None, None, None]
    device_index = jnp.arange(device_count, dtype=jnp.int32)[None, :, None, None]
    round_span = round_index + (owner_ids < device_index).astype(jnp.int32)
    picked = jax.random.randint(round_key, owner_ids.shape, 0, jnp.maximum(round_span, 1), dtype=jnp.int32)
    return jnp.where(round_span > 0, picked * device_count + owner_ids, -1).astype(jnp.int32)


def block_levels(own_key, shape, pieces, least, top_value):
    level = 1.0
    for dim, shards_of in pieces:
        heights = jax.random.uniform(jax.random.fold_in(jax.random.fold_in(own_key, 6), dim), (shards_of,), jnp.float32, least / len(pieces), top_value / len(pieces))
        level = level * jnp.repeat(jnp.exp(heights), shape[dim] // shards_of).reshape((-1,) + (1,) * (len(shape) - 1 - dim))
    return level


def gaussian(key, dims, scale, most, cuts=(), held_as=jnp.bfloat16):
    entries = scale * jax.random.normal(key, dims, jnp.float32)
    if cuts:
        entries = entries * block_levels(key, dims, cuts, -0.22, 0.18)
    return jnp.clip(entries, -most, most).astype(held_as)


def setup_inputs(seed: int = 0) -> dict:
    key_list = jax.random.split(jax.random.key(seed), 8)
    query_states = draw_query_states(jax.random.fold_in(key_list[7], 71), 0)
    key_states = draw_key_states(jax.random.fold_in(key_list[7], 71), 0)
    value_states = gaussian(key_list[2], (R, ROUND_TOKENS, KVH * HD), 1.0, 6.0, ((1, 128),))
    forward_out = gaussian(key_list[3], (R, ROUND_TOKENS, QH * HD), 0.5, 4.0, ((1, 128),))
    out_grad = draw_out_grad(jax.random.fold_in(key_list[7], 71), 0)
    log_norm = jnp.clip(3.0 + 2.0 * jax.random.uniform(key_list[5], (R, ROUND_TOKENS, QH), jnp.float32) ** block_levels(key_list[5], (R, ROUND_TOKENS, QH), ((1, 128),), -0.2, 0.2), 3.0, 5.0)
    selected = draw_selected(jax.random.fold_in(key_list[7], 71), 0)
    return dict(query_states=query_states, key_states=key_states, value_states=value_states, forward_out=forward_out, out_grad=out_grad, log_norm=log_norm, selected=selected)


def list_terms(query_rows, grad_rows, norm_rows, delta_rows, key_rows, value_rows, visible, softmax_scale):
    contract_last = (((1,), (1,)), ((), ()))
    contract_first = (((0,), (0,)), ((), ()))
    scores = lax.dot_general(query_rows, key_rows, contract_last, preferred_element_type=jnp.float32) * softmax_scale
    weights = jnp.where(visible, jnp.exp(scores - norm_rows[:, None]), jnp.float32(0.0))
    grad_weights = lax.dot_general(grad_rows, value_rows, contract_last, preferred_element_type=jnp.float32)
    grad_scores = weights * (grad_weights - delta_rows[:, None])
    weights_low = weights.astype(jnp.bfloat16)
    scores_low = grad_scores.astype(jnp.bfloat16)
    query_part = jnp.dot(scores_low, key_rows, preferred_element_type=jnp.float32) * softmax_scale
    key_part = lax.dot_general(scores_low, query_rows, contract_first, preferred_element_type=jnp.float32) * softmax_scale
    value_part = lax.dot_general(weights_low, grad_rows, contract_first, preferred_element_type=jnp.float32)
    return query_part, key_part, value_part


def reference(query_states, key_states, value_states, forward_out, out_grad, log_norm, selected):
    round_blocks = N_CTX * N_WORK
    block_count = R * round_blocks
    head_count = GQ * KVH
    softmax_scale = HD ** -0.5
    query_blocks = query_states.reshape(block_count, BLK, head_count * HD)
    grad_blocks = out_grad.reshape(block_count, BLK, head_count * HD)
    output_blocks = forward_out.reshape(block_count, BLK, head_count * HD)
    norm_blocks = log_norm.reshape(block_count, BLK, head_count)
    key_blocks = key_states.reshape(block_count, BLK, KVH, HD)
    value_blocks = value_states.reshape(block_count, BLK, KVH, HD)
    sel_blocks = selected.reshape(block_count, KVH, NSEL)
    row_token = jnp.arange(BLK * GQ, dtype=jnp.int32) // GQ
    causal = jnp.arange(BLK, dtype=jnp.int32)[None, :] <= row_token[:, None]

    def block_step(totals, block_index):
        key_acc, value_acc = totals
        query_block = query_blocks[block_index]
        grad_block = grad_blocks[block_index]
        output_block = output_blocks[block_index]
        norm_block = norm_blocks[block_index]
        delta_block = jnp.sum((grad_block.astype(jnp.float32) * output_block.astype(jnp.float32)).reshape(BLK, head_count, HD), axis=-1)
        query_parts = []
        for kv_head in range(KVH):
            chosen = sel_blocks[block_index, kv_head]
            present = chosen >= 0
            safe_index = jnp.maximum(chosen, 0).astype(jnp.int32)
            key_rows = jnp.concatenate([key_blocks[block_index, :, kv_head], key_blocks[safe_index, :, kv_head].reshape(NSEL * BLK, HD)], axis=0)
            value_rows = jnp.concatenate([value_blocks[block_index, :, kv_head], value_blocks[safe_index, :, kv_head].reshape(NSEL * BLK, HD)], axis=0)
            far_visible = jnp.broadcast_to(jnp.repeat(present, BLK)[None, :], (BLK * GQ, NSEL * BLK))
            visible = jnp.concatenate([causal, far_visible], axis=1)
            head_start = kv_head * GQ * HD
            query_rows = query_block[:, head_start:head_start + GQ * HD].reshape(BLK * GQ, HD)
            grad_rows = grad_block[:, head_start:head_start + GQ * HD].reshape(BLK * GQ, HD)
            norm_rows = norm_block[:, kv_head * GQ:(kv_head + 1) * GQ].reshape(BLK * GQ)
            delta_rows = delta_block[:, kv_head * GQ:(kv_head + 1) * GQ].reshape(BLK * GQ)
            query_part, key_part, value_part = list_terms(query_rows, grad_rows, norm_rows, delta_rows, key_rows, value_rows, visible, softmax_scale)
            query_parts.append(query_part.reshape(BLK, GQ * HD))
            key_acc = key_acc.at[block_index, :, kv_head].add(key_part[:BLK])
            key_acc = key_acc.at[safe_index, :, kv_head].add(key_part[BLK:].reshape(NSEL, BLK, HD))
            value_acc = value_acc.at[block_index, :, kv_head].add(value_part[:BLK])
            value_acc = value_acc.at[safe_index, :, kv_head].add(value_part[BLK:].reshape(NSEL, BLK, HD))
        return (key_acc, value_acc), jnp.concatenate(query_parts, axis=1).astype(jnp.bfloat16)

    empty_grads = jnp.zeros((block_count, BLK, KVH, HD), jnp.float32)
    (key_acc, value_acc), query_grad = lax.scan(block_step, (empty_grads, empty_grads), jnp.arange(block_count, dtype=jnp.int32))
    return (query_grad.reshape(R, round_blocks * BLK, head_count * HD),
            key_acc.astype(jnp.bfloat16).reshape(R, round_blocks * BLK, KVH * HD),
            value_acc.astype(jnp.bfloat16).reshape(R, round_blocks * BLK, KVH * HD))
```

```python
import functools
import math

import jax
import jax.numpy as jnp
from jax import lax
from jax.experimental import pallas as pl
from jax.experimental.pallas import tpu as pltpu
from jax.sharding import PartitionSpec as P

HD = 128
KVH = 2
GQ = 16
BLK = 64
NSEL = 15
ROWS = GQ * BLK
SCALE = HD**-0.5
LOG2E = math.log2(math.e)
NT = (((1,), (1,)), ((), ()))
NN = (((1,), (0,)), ((), ()))
TN = (((0,), (0,)), ((), ()))
VMEM_LIMIT = 48 * 1024 * 1024


def dot(a, b, dims):
    return lax.dot_general(a, b, dims, preferred_element_type=jnp.float32)


def head_rows(ref):
    return jnp.concatenate([ref[:, h * HD : (h + 1) * HD] for h in range(GQ)], axis=0)


def terms(keys, values, q, do, norm, delta, visible=None):
    s = dot(keys, q, NT)
    p = jnp.exp2(s * (SCALE * LOG2E) - norm)
    if visible is not None:
        p = jnp.where(visible, p, 0.0)
    ds = p * (dot(values, do, NT) - delta)
    return p.astype(jnp.bfloat16), ds.astype(jnp.bfloat16)


def causal_mask():
    key = lax.broadcasted_iota(jnp.int32, (BLK, ROWS), 0)
    row = lax.broadcasted_iota(jnp.int32, (BLK, ROWS), 1)
    return key <= lax.rem(row, BLK)


def request_kernel(sel_ref, out_ref):
    out_ref[...] = jnp.full(out_ref.shape, -1, jnp.int32)
    for item in range(sel_ref.shape[0]):
        head = item // NSEL % KVH
        block = sel_ref[item]

        @pl.when(block >= 0)
        def _():
            owner = lax.rem(block, out_ref.shape[0])
            code = lax.div(block, out_ref.shape[0]) * KVH + head
            out_ref[owner] = jnp.full(out_ref.shape[1:], code, jnp.int32)


def build_request(flat_sel, devices):
    return pl.pallas_call(
        request_kernel,
        out_shape=jax.ShapeDtypeStruct((devices, 1, 128), jnp.int32),
        in_specs=[pl.BlockSpec(memory_space=pltpu.SMEM)],
        out_specs=pl.BlockSpec(memory_space=pltpu.VMEM),
        name="request",
    )(flat_sel)


PACK = 16


def pack_kernel(wanted_ref, key_ref, value_ref, out_ref, table):
    step = pl.program_id(0)

    @pl.when(step == 0)
    def _():
        for r in range(key_ref.shape[0]):
            for g in range(KVH):
                table[r * KVH + g, :, :HD] = key_ref[r, :, g * HD : (g + 1) * HD]
                table[r * KVH + g, :, HD:] = value_ref[r, :, g * HD : (g + 1) * HD]

    for i in range(PACK):
        code = jnp.maximum(wanted_ref[step * PACK + i, 0, 0], 0)
        out_ref[i] = table[code]


def pack(wanted, key_states, value_states):
    devices = wanted.shape[0]
    rounds = key_states.shape[0]
    return pl.pallas_call(
        pack_kernel,
        grid=(devices // PACK,),
        out_shape=jax.ShapeDtypeStruct((devices, BLK, 2 * HD), jnp.bfloat16),
        in_specs=[
            pl.BlockSpec(memory_space=pltpu.SMEM),
            pl.BlockSpec(key_states.shape, lambda i: (0, 0, 0)),
            pl.BlockSpec(key_states.shape, lambda i: (0, 0, 0)),
        ],
        out_specs=pl.BlockSpec((PACK, BLK, 2 * HD), lambda i: (i, 0, 0)),
        scratch_shapes=[pltpu.VMEM((rounds * KVH, BLK, 2 * HD), jnp.bfloat16)],
        name="pack",
    )(wanted, key_states, value_states)


def near_kernel(q_ref, do_ref, stat_ref, key_ref, value_ref, out_ref):
    q = head_rows(q_ref)
    do = head_rows(do_ref)
    p, ds = terms(
        key_ref[...], value_ref[...], q, do, stat_ref[0:1], stat_ref[1:2], causal_mask()
    )
    out_ref[:, :HD] = dot(ds, q, NN) * SCALE
    out_ref[:, HD:] = dot(p, do, NN)


def row_specs():
    wide = pl.BlockSpec((None, BLK, GQ * HD), lambda l, *_: (l // KVH, 0, l % KVH))
    stat = pl.BlockSpec((None, 2, ROWS), lambda l, *_: (l, 0, 0))
    own = pl.BlockSpec((None, BLK, HD), lambda l, *_: (l // KVH, 0, l % KVH))
    return wide, stat, own


def near(query_states, out_grad, stats, key_states, value_states):
    lists = stats.shape[0]
    wide, stat, own = row_specs()
    flops = lists * 4 * BLK * ROWS * HD * 2
    return pl.pallas_call(
        near_kernel,
        grid=(lists,),
        out_shape=jax.ShapeDtypeStruct((lists, BLK, 2 * HD), jnp.float32),
        in_specs=[wide, wide, stat, own, own],
        out_specs=pl.BlockSpec((None, BLK, 2 * HD), lambda l: (l, 0, 0)),
        compiler_params=pltpu.CompilerParams(vmem_limit_bytes=VMEM_LIMIT),
        cost_estimate=pl.CostEstimate(
            flops=flops, bytes_accessed=5 << 20, transcendentals=lists * BLK * ROWS
        ),
        name="near",
    )(query_states, out_grad, stats, key_states, value_states)


def got_copy(sel_ref, got_ref, buf, sem, lst, slot, s):
    owner = jnp.maximum(sel_ref[lst * NSEL + s], 0) & (got_ref.shape[0] - 1)
    return pltpu.make_async_copy(
        got_ref.at[owner], buf.at[slot, pl.ds(s * BLK, BLK)], sem.at[slot, s]
    )


def fetch_lists(sel_ref, got_ref, buf, sem):
    lst = pl.program_id(0)
    slot = lax.rem(lst, 2)

    @pl.when(lst == 0)
    def _():
        for s in range(NSEL):
            got_copy(sel_ref, got_ref, buf, sem, 0, 0, s).start()

    @pl.when(lst + 1 < pl.num_programs(0))
    def _():
        for s in range(NSEL):
            got_copy(sel_ref, got_ref, buf, sem, lst + 1, 1 - slot, s).start()

    for s in range(NSEL):
        got_copy(sel_ref, got_ref, buf, sem, lst, slot, s).wait()
    return lst, slot


FAR_TILE = 5


def far_kernel(sel_ref, q_ref, do_ref, stat_ref, got_ref, out_ref, buf, sem, res, out_sem):
    lst, slot = fetch_lists(sel_ref, got_ref, buf, sem)

    def for_items(which, where, act):
        for s in range(NSEL):
            block = sel_ref[which * NSEL + s]

            @pl.when(block >= 0)
            def _():
                act(
                    pltpu.make_async_copy(
                        res.at[where, pl.ds(s * BLK, BLK)],
                        out_ref.at[block & (out_ref.shape[0] - 1)],
                        out_sem.at[where, s],
                    )
                )

    @pl.when(lst >= 2)
    def _():
        for_items(lst - 2, slot, lambda c: c.wait())

    q = head_rows(q_ref)
    do = head_rows(do_ref)
    norm, delta = stat_ref[0:1], stat_ref[1:2]
    tile = FAR_TILE * BLK
    for t in range(NSEL // FAR_TILE):
        rows = pl.ds(t * tile, tile)
        p, ds = terms(buf[slot, rows, :HD], buf[slot, rows, HD:], q, do, norm, delta)
        res[slot, rows, :HD] = (dot(ds, q, NN) * SCALE).astype(jnp.bfloat16)
        res[slot, rows, HD:] = dot(p, do, NN).astype(jnp.bfloat16)
    for_items(lst, slot, lambda c: c.start())

    @pl.when(lst == pl.num_programs(0) - 1)
    def _():
        for_items(lst - 1, 1 - slot, lambda c: c.wait())
        for_items(lst, slot, lambda c: c.wait())


def far(flat_sel, query_states, out_grad, stats, got):
    lists = stats.shape[0]
    wide, stat, _ = row_specs()
    keys = NSEL * BLK
    return pl.pallas_call(
        far_kernel,
        grid_spec=pltpu.PrefetchScalarGridSpec(
            num_scalar_prefetch=1,
            grid=(lists,),
            in_specs=[wide, wide, stat, pl.BlockSpec(memory_space=pl.ANY)],
            out_specs=pl.BlockSpec(memory_space=pl.ANY),
            scratch_shapes=[
                pltpu.VMEM((2, keys, 2 * HD), jnp.bfloat16),
                pltpu.SemaphoreType.DMA((2, NSEL)),
                pltpu.VMEM((2, keys, 2 * HD), jnp.bfloat16),
                pltpu.SemaphoreType.DMA((2, NSEL)),
            ],
        ),
        out_shape=jax.ShapeDtypeStruct(got.shape, jnp.bfloat16),
        compiler_params=pltpu.CompilerParams(vmem_limit_bytes=VMEM_LIMIT),
        cost_estimate=pl.CostEstimate(
            flops=lists * 4 * keys * ROWS * HD * 2,
            bytes_accessed=12 << 20,
            transcendentals=lists * keys * ROWS,
        ),
        name="far",
    )(flat_sel, query_states, out_grad, stats, got)


def query_kernel(
    sel_ref, q_ref, do_ref, stat_ref, key_ref, value_ref, got_ref, out_ref, buf, sem
):
    lst, slot = fetch_lists(sel_ref, got_ref, buf, sem)
    for s in range(NSEL):

        @pl.when(sel_ref[lst * NSEL + s] < 0)
        def _():
            buf[slot, pl.ds(s * BLK, BLK)] = jnp.zeros((BLK, 2 * HD), jnp.bfloat16)

    q = head_rows(q_ref)
    do = head_rows(do_ref)
    norm, delta = stat_ref[0:1], stat_ref[1:2]
    keys = key_ref[...]
    _, ds = terms(keys, value_ref[...], q, do, norm, delta, causal_mask())
    total = dot(keys, ds, TN)
    tile = FAR_TILE * BLK
    for t in range(NSEL // FAR_TILE):
        rows = pl.ds(t * tile, tile)
        keys = buf[slot, rows, :HD]
        _, ds = terms(keys, buf[slot, rows, HD:], q, do, norm, delta)
        total += dot(keys, ds, TN)
    total = (total * SCALE).T.astype(jnp.bfloat16)
    for h in range(GQ):
        out_ref[:, h * HD : (h + 1) * HD] = total[h * BLK : (h + 1) * BLK]


def query_terms(flat_sel, query_states, out_grad, stats, key_states, value_states, got):
    lists = stats.shape[0]
    wide, stat, own = row_specs()
    keys = NSEL * BLK
    return pl.pallas_call(
        query_kernel,
        grid_spec=pltpu.PrefetchScalarGridSpec(
            num_scalar_prefetch=1,
            grid=(lists,),
            in_specs=[wide, wide, stat, own, own, pl.BlockSpec(memory_space=pl.ANY)],
            out_specs=wide,
            scratch_shapes=[
                pltpu.VMEM((2, keys, 2 * HD), jnp.bfloat16),
                pltpu.SemaphoreType.DMA((2, NSEL)),
            ],
        ),
        out_shape=jax.ShapeDtypeStruct(query_states.shape, jnp.bfloat16),
        compiler_params=pltpu.CompilerParams(vmem_limit_bytes=VMEM_LIMIT),
        cost_estimate=pl.CostEstimate(
            flops=lists * 3 * (keys + BLK) * ROWS * HD * 2,
            bytes_accessed=12 << 20,
            transcendentals=lists * (keys + BLK) * ROWS,
        ),
        name="query_terms",
    )(flat_sel, query_states, out_grad, stats, key_states, value_states, got)


SUM_TOKENS = 16


def sum_kernel(wanted_ref, back_ref, own_ref, key_out, value_out, acc):
    lists = own_ref.shape[0]
    acc[:lists] = own_ref[...]

    def add(d, carry):
        code = wanted_ref[d, 0, 0]
        code = jnp.where(code < 0, lists, code)
        acc[code] += back_ref[d].astype(jnp.float32)
        return carry

    lax.fori_loop(0, back_ref.shape[0], add, 0, unroll=8)
    for l in range(lists):
        r, g = l // KVH, l % KVH
        key_out[r, :, g * HD : (g + 1) * HD] = acc[l, :, :HD].astype(jnp.bfloat16)
        value_out[r, :, g * HD : (g + 1) * HD] = acc[l, :, HD:].astype(jnp.bfloat16)


def sum_back(wanted, back, own):
    lists = own.shape[0]
    rounds = lists // KVH
    devices = back.shape[0]
    out = jax.ShapeDtypeStruct((rounds, BLK, KVH * HD), jnp.bfloat16)
    out_spec = pl.BlockSpec((rounds, SUM_TOKENS, KVH * HD), lambda i: (0, i, 0))
    return pl.pallas_call(
        sum_kernel,
        grid=(BLK // SUM_TOKENS,),
        out_shape=(out, out),
        in_specs=[
            pl.BlockSpec(memory_space=pltpu.SMEM),
            pl.BlockSpec((devices, SUM_TOKENS, 2 * HD), lambda i: (0, i, 0)),
            pl.BlockSpec((lists, SUM_TOKENS, 2 * HD), lambda i: (0, i, 0)),
        ],
        out_specs=(out_spec, out_spec),
        scratch_shapes=[pltpu.VMEM((lists + 1, SUM_TOKENS, 2 * HD), jnp.float32)],
        compiler_params=pltpu.CompilerParams(vmem_limit_bytes=VMEM_LIMIT),
        name="sum_back",
    )(wanted, back, own)


def swap(x):
    return lax.all_to_all(x, ("ctx", "work"), split_axis=0, concat_axis=0, tiled=True)


def by_list(x):
    return jnp.transpose(x, (0, 2, 1)).reshape(x.shape[0] * KVH, ROWS)


def shards(query_states, key_states, value_states, forward_out, out_grad, log_norm, selected):
    devices = lax.axis_size(("ctx", "work"))
    rounds = query_states.shape[0]
    flat_sel = selected.reshape(rounds * KVH * NSEL)

    wanted = swap(build_request(flat_sel, devices))
    got = swap(pack(wanted, key_states, value_states))

    delta = jnp.sum(
        (out_grad.astype(jnp.float32) * forward_out.astype(jnp.float32)).reshape(
            rounds, BLK, KVH * GQ, HD
        ),
        axis=-1,
    )
    stats = jnp.stack([by_list(log_norm * LOG2E), by_list(delta)], axis=1)
    own = near(query_states, out_grad, stats, key_states, value_states)

    back = swap(far(flat_sel, query_states, out_grad, stats, got))
    query_grad = query_terms(
        flat_sel, query_states, out_grad, stats, key_states, value_states, got
    )
    key_grad, value_grad = sum_back(wanted, back, own)
    return query_grad, key_grad, value_grad


def solution(mesh):
    split = P(None, ("ctx", "work"), None)
    return jax.shard_map(
        shards,
        mesh=mesh,
        in_specs=(split,) * 6 + (P(None, ("ctx", "work"), None, None),),
        out_specs=(split,) * 3,
        check_vma=False,
    )
```
